32 devices in a mesh: dp: 2 (over y), expert: 4 (over x, core), hid: 4 (over z).
Axes of the slice: x: 2, y: 2, z: 4, core: 2. Of those that a mesh axis runs over, the one named last changes fastest.
Arguments:
- images_in: bfloat16 [32, 256, 1024], P(('dp', 'expert', 'hid')), may hold values from -16 to 16
- slot_keys: bfloat16 [1024, 16], replicated, may hold values from -6 to 6
- w_in: bfloat16 [8, 1024, 4096], P('expert', None, 'hid'), may hold values from -0.1875 to 0.1875
- w_out: bfloat16 [8, 4096, 1024], P('expert', 'hid'), may hold values from -0.09375 to 0.09375
Outputs:
- mixed: bfloat16 [32, 256, 1024], P(('dp', 'expert', 'hid'))
The draws below stay inside these ranges and needn't reach their ends.
All inputs are finite; a program needn't handle non-finite values.
Results may differ from the reference program's by a relative error of at most 0.013.
Values may be sent and summed in bfloat16 or wider, within the bound.
A program may use at most 64 MiB of HBM per device.

```python
import jax
import jax.numpy as jnp
from jax import lax

D = 1024
FF = 4096
SLOTS = 2
TOK = 256
EXPERTS = 8
IMAGES = 32
N_HID = 4


def block_levels(stream_key, extent, cuts, smallest, top_value):
    def one(position, blocks):
        draws = jax.random.uniform(jax.random.fold_in(jax.random.fold_in(stream_key, 6), position), (blocks,), jnp.float32, smallest / len(cuts), top_value / len(cuts))
        return jnp.repeat(jnp.exp(draws), extent[position] // blocks).reshape((-1,) + (1,) * (len(extent) - position - 1))

    level = one(*cuts[0])
    for cut in cuts[1:]:
        level = level * one(*cut)
    return level


def gaussian(rng, extent, spread, reach, shards=(), kind=jnp.bfloat16):
    drawn = spread * jax.random.normal(rng, extent, jnp.float32)
    if shards:
        drawn = drawn * block_levels(rng, extent, shards, -0.22, 0.18)
    return jnp.clip(drawn, -reach, reach).astype(kind)


def setup_inputs(seed: int = 0) -> dict:
    key_of = jax.random.split(jax.random.key(seed), 5)
    images_in = gaussian(key_of[0], (IMAGES, TOK, D), 3.0, 16.0, ((0, 32),))
    slot_keys = gaussian(key_of[1], (D, EXPERTS * SLOTS), 1.0, 6.0)
    w_in = gaussian(key_of[2], (EXPERTS, D, FF), D ** -0.5, 0.1875, ((0, 4), (2, 4)))
    w_out = gaussian(key_of[3], (EXPERTS, FF, D), FF ** -0.5, 0.09375, ((0, 4), (1, 4)))
    return dict(images_in=images_in, slot_keys=slot_keys, w_in=w_in, w_out=w_out)


def normal_rows(values):
    floats = values.astype(jnp.float32)
    return (floats * lax.rsqrt(lax.optimization_barrier(jnp.mean(floats * floats, axis=-1, keepdims=True)) + 1e-06)).astype(jnp.bfloat16)

def unit_columns(values):
    floats = values.astype(jnp.float32)
    return (floats * lax.rsqrt(lax.optimization_barrier(jnp.sum(floats * floats, axis=0, keepdims=True)) + 1e-06)).astype(jnp.bfloat16)

def reference(images_in, slot_keys, w_in, w_out):
    unit_keys = unit_columns(slot_keys)

    def mix_image(tokens):
        normed = normal_rows(tokens)
        logits = 2.0 * jnp.dot(normed, unit_keys, preferred_element_type=jnp.float32)
        powers = jnp.exp(logits)
        dispatch = (powers / lax.optimization_barrier(jnp.sum(powers, axis=0, keepdims=True))).astype(jnp.bfloat16)
        combine = (powers / lax.optimization_barrier(jnp.sum(powers, axis=1, keepdims=True))).astype(jnp.bfloat16)
        slot_in = lax.dot_general(dispatch, tokens, (((0,), (0,)), ((), ())), preferred_element_type=jnp.float32)
        return (slot_in.astype(jnp.bfloat16), combine)
    slot_in, combine = lax.map(mix_image, images_in)
    grouped = slot_in.reshape(IMAGES, EXPERTS, SLOTS, D)
    quarter = FF // N_HID

    def run_expert(expert_id):
        slot_rows = lax.dynamic_index_in_dim(grouped, expert_id, 1, keepdims=False)
        slot_rows = slot_rows.reshape(IMAGES * SLOTS, D).astype(jnp.float32)
        w_first = lax.dynamic_index_in_dim(w_in, expert_id, 0, keepdims=False).astype(jnp.float32).reshape(D, N_HID, quarter)
        w_second = lax.dynamic_index_in_dim(w_out, expert_id, 0, keepdims=False).astype(jnp.float32).reshape(N_HID, quarter, D)
        hidden = jax.nn.gelu(jnp.einsum('rd,dqf->rqf', slot_rows, w_first), approximate=True).astype(jnp.bfloat16)
        partial_value = jnp.einsum('rqf,qfd->rqd', hidden.astype(jnp.float32), w_second).astype(jnp.bfloat16)
        return lax.optimization_barrier(jnp.sum(partial_value.astype(jnp.float32), axis=1)).astype(jnp.bfloat16)
    slot_out = lax.map(run_expert, jnp.arange(EXPERTS, dtype=jnp.int32))
    slot_out = slot_out.reshape(EXPERTS, IMAGES, SLOTS, D).transpose(1, 0, 2, 3).reshape(IMAGES, EXPERTS * SLOTS, D)

    def combine_image(paired):
        return jnp.dot(paired[0], paired[1], preferred_element_type=jnp.float32).astype(jnp.bfloat16)
    return lax.map(combine_image, (combine, slot_out))
```

```python
import functools

import jax
import jax.numpy as jnp
from jax import lax
from jax.experimental import pallas as pl
from jax.experimental.pallas import tpu as pltpu
from jax.sharding import PartitionSpec as P

SLOTS = 2
LANES = 128
ROWS = 16
MESH = pl.DeviceIdType.MESH


def each(count, step):
    if count <= 16:
        for s in range(1, count):
            step(s)
    else:

        def one(s, carry):
            step(s)
            return carry

        lax.fori_loop(1, count, one, 0)


def one_hot(hit):
    return jnp.where(hit, 1.0, 0.0).astype(jnp.bfloat16)


def dot(a, b, dims=((1,), (0,))):
    return lax.dot_general(a, b, (dims, ((), ())), preferred_element_type=jnp.float32)


def kernel(
    owners,
    shares,
    x_hbm,
    keys_hbm,
    w_in_hbm,
    w_out_hbm,
    out,
    x_v,
    keys_v,
    w_in_v,
    w_out_v,
    send_in,
    recv_in,
    send_out,
    recv_out,
    spread_v,
    local_sem,
    send_sem,
    recv_sem,
):
    peers = owners * shares
    tokens, width = x_v.shape
    experts, _, units = w_in_v.shape
    own = experts * SLOTS
    columns = keys_v.shape[0]
    fold = ROWS // own
    part = width // fold
    me_e = lax.axis_index("expert")
    me_h = lax.axis_index("hid")
    me = me_e * shares + me_h

    x_copy = pltpu.make_async_copy(x_hbm.at[0], x_v, local_sem.at[0])
    keys_copy = pltpu.make_async_copy(keys_hbm, keys_v, local_sem.at[1])
    x_copy.start()
    keys_copy.start()

    def peer(s):
        p = lax.rem(me + s, peers)
        e = lax.div(p, shares)
        return p, e, {"expert": e, "hid": lax.rem(p, shares)}

    barrier = pltpu.get_barrier_semaphore()

    def greet(s):
        pl.semaphore_signal(barrier, inc=1, device_id=peer(s)[2], device_id_type=MESH)

    each(peers, greet)

    keys_copy.wait()
    keys = keys_v[...].astype(jnp.float32)
    unit = (keys * lax.rsqrt(jnp.sum(keys * keys, axis=1, keepdims=True) + 1e-06)).astype(
        jnp.bfloat16
    )
    x_copy.wait()
    weights = []
    for e in range(experts):
        for k, (hbm, vmem) in enumerate(((w_in_hbm, w_in_v), (w_out_hbm, w_out_v))):
            weights.append(
                pltpu.make_async_copy(hbm.at[e], vmem.at[e], local_sem.at[2 + 2 * e + k])
            )
    for copy in weights[0::2] + weights[1::2]:
        copy.start()

    x = x_v[...]
    logits = dot(unit, x, ((1,), (1,)))
    squares = None
    for start in range(0, width, LANES):
        floats = x[:, start : start + LANES].astype(jnp.float32)
        squares = floats * floats if squares is None else squares + floats * floats
    high = squares.astype(jnp.bfloat16)
    low = (squares - high.astype(jnp.float32)).astype(jnp.bfloat16)
    ones = jnp.ones((ROWS, LANES), jnp.bfloat16)
    total = dot(ones, high, ((1,), (1,))) + dot(ones, low, ((1,), (1,)))
    scale = 2.0 * lax.rsqrt(total[0:1] * (1.0 / width) + 1e-06)
    powers = jnp.exp(logits * scale)
    dispatch = (powers / jnp.sum(powers, axis=1, keepdims=True)).astype(jnp.bfloat16)
    slot_in = dot(dispatch, x)

    def message(values, first):
        return jnp.concatenate(
            [
                values[first : first + own, k * part : (k + 1) * part]
                for k in range(fold)
            ],
            axis=0,
        ).astype(jnp.bfloat16)

    for e in range(owners):
        send_in[e] = message(slot_in, e * own)
    pl.semaphore_wait(barrier, peers - 1)

    def send_slots(s):
        _, e, device = peer(s)
        pltpu.make_async_remote_copy(
            src_ref=send_in.at[e],
            dst_ref=recv_in.at[me],
            send_sem=send_sem.at[0],
            recv_sem=recv_sem.at[0],
            device_id=device,
            device_id_type=MESH,
        ).start()

    each(peers, send_slots)
    recv_in[me] = send_in[me_e]

    combine = (powers / jnp.sum(powers, axis=0, keepdims=True)).astype(jnp.bfloat16)
    col = lax.broadcasted_iota(jnp.int32, (columns, peers * ROWS), 0)
    row = lax.broadcasted_iota(jnp.int32, (columns, peers * ROWS), 1)
    col_hit = col == (row // (ROWS * shares)) * own + row % own
    for k in range(fold):
        hit = jnp.logical_and(col_hit, (row // own) % fold == k)
        spread_v[k] = dot(combine, one_hot(hit), ((0,), (0,))).astype(jnp.bfloat16)

    group = min(peers, 16)
    block = group * ROWS

    def by_expert(axis):
        to = lax.broadcasted_iota(jnp.int32, (block, block), axis)
        at = lax.broadcasted_iota(jnp.int32, (block, block), 1 - axis)
        slot = to % SLOTS
        image = (to // SLOTS) % group
        rest = to // (SLOTS * group)
        return one_hot(at == image * ROWS + rest * SLOTS + slot)

    sort = by_expert(0)
    unsort = by_expert(1)

    def all_but_one(buffer, sem):
        view = buffer.at[pl.ds(0, peers - 1)]
        return pltpu.make_async_copy(view, view, sem)

    all_but_one(recv_in, recv_sem.at[0]).wait()

    groups = peers // group
    span = group * SLOTS
    sorted_rows = [
        dot(sort, recv_in[g * group : (g + 1) * group].reshape(block, part)).astype(jnp.bfloat16)
        for g in range(groups)
    ]
    partial = []
    for e in range(experts):
        weights[2 * e].wait()
        hidden = None
        for k in range(fold):
            start = (k * experts + e) * span
            rows = jnp.concatenate([r[start : start + span] for r in sorted_rows], axis=0)
            term = dot(rows, w_in_v[e, k * part : (k + 1) * part, :])
            hidden = term if hidden is None else hidden + term
        hidden = jax.nn.gelu(hidden, approximate=True).astype(jnp.bfloat16)
        weights[2 * e + 1].wait()
        partial.append(dot(hidden, w_out_v[e]).astype(jnp.bfloat16))
    for g in range(groups):
        rows = jnp.concatenate(
            [
                partial[e][g * span : (g + 1) * span, k * part : (k + 1) * part]
                for k in range(fold)
                for e in range(experts)
            ],
            axis=0,
        )
        send_out[g * group : (g + 1) * group] = (
            dot(unsort, rows).astype(jnp.bfloat16).reshape(group, ROWS, part)
        )

    def send_results(s):
        p, _, device = peer(s)
        pltpu.make_async_remote_copy(
            src_ref=send_out.at[p],
            dst_ref=recv_out.at[me],
            send_sem=send_sem.at[1],
            recv_sem=recv_sem.at[1],
            device_id=device,
            device_id_type=MESH,
        ).start()

    each(peers, send_results)
    recv_out[me] = send_out[me]
    all_but_one(recv_in, send_sem.at[0]).wait()
    all_but_one(recv_out, recv_sem.at[1]).wait()
    arrived = recv_out[...].reshape(peers * ROWS, part)
    for k in range(fold):
        out[0, :, k * part : (k + 1) * part] = dot(spread_v[k], arrived).astype(out.dtype)
    all_but_one(send_out, send_sem.at[1]).wait()


def body(images_in, slot_keys, w_in, w_out):
    owners = lax.axis_size("expert")
    shares = lax.axis_size("hid")
    peers = owners * shares
    _, tokens, width = images_in.shape
    own = w_in.shape[0] * SLOTS
    fold = ROWS // own
    part = width // fold
    hbm = pl.BlockSpec(memory_space=pltpu.HBM)
    bf16 = jnp.bfloat16
    return pl.pallas_call(
        functools.partial(kernel, owners, shares),
        out_shape=jax.ShapeDtypeStruct(images_in.shape, bf16),
        in_specs=[hbm] * 4,
        out_specs=pl.BlockSpec(memory_space=pltpu.VMEM),
        scratch_shapes=[
            pltpu.VMEM((tokens, width), bf16),
            pltpu.VMEM(slot_keys.shape[::-1], bf16),
            pltpu.VMEM(w_in.shape, bf16),
            pltpu.VMEM(w_out.shape, bf16),
            pltpu.VMEM((owners, ROWS, part), bf16),
            pltpu.VMEM((peers, ROWS, part), bf16),
            pltpu.VMEM((peers, ROWS, part), bf16),
            pltpu.VMEM((peers, ROWS, part), bf16),
            pltpu.VMEM((fold, tokens, peers * ROWS), bf16),
            pltpu.SemaphoreType.DMA((2 + 2 * w_in.shape[0],)),
            pltpu.SemaphoreType.DMA((2,)),
            pltpu.SemaphoreType.DMA((2,)),
        ],
        compiler_params=pltpu.CompilerParams(
            collective_id=0, has_side_effects=True, vmem_limit_bytes=60 * 1024 * 1024
        ),
    )(images_in, slot_keys.T, w_in, w_out)


def solution(mesh):
    return jax.shard_map(
        body,
        mesh=mesh,
        in_specs=(
            P(("dp", "expert", "hid"), None, None),
            P(),
            P("expert", None, "hid"),
            P("expert", "hid", None),
        ),
        out_specs=P(("dp", "expert", "hid"), None, None),
        check_vma=False,
    )
```

```python
import functools

import jax
import jax.numpy as jnp
from jax import lax
from jax.experimental import pallas as pl
from jax.experimental.pallas import tpu as pltpu
from jax.sharding import PartitionSpec as P

SLOTS = 2
LANES = 128
ROWS = 16
MESH = pl.DeviceIdType.MESH


def each(count, step):
    if count <= 16:
        for s in range(1, count):
            step(s)
    else:

        def one(s, carry):
            step(s)
            return carry

        lax.fori_loop(1, count, one, 0)


def one_hot(hit):
    return jnp.where(hit, 1.0, 0.0).astype(jnp.bfloat16)


def dot(a, b, dims=((1,), (0,))):
    return lax.dot_general(a, b, (dims, ((), ())), preferred_element_type=jnp.float32)


def kernel(
    owners,
    shares,
    x_hbm,
    keys_hbm,
    w_in_hbm,
    w_out_hbm,
    out,
    x_v,
    keys_v,
    w_in_v,
    w_out_v,
    send_in,
    recv_in,
    send_out,
    recv_out,
    spread_v,
    local_sem,
    send_sem,
    recv_sem,
):
    peers = owners * shares
    tokens, width = x_v.shape
    experts, _, units = w_in_v.shape
    own = experts * SLOTS
    columns = keys_v.shape[0]
    fold = ROWS // own
    part = width // fold
    me_e = lax.axis_index("expert")
    me_h = lax.axis_index("hid")
    me = me_h * owners + me_e

    x_copy = pltpu.make_async_copy(x_hbm.at[0], x_v, local_sem.at[0])
    keys_copy = pltpu.make_async_copy(keys_hbm, keys_v, local_sem.at[1])
    x_copy.start()
    keys_copy.start()

    def at(p):
        return {"expert": lax.rem(p, owners), "hid": lax.div(p, owners)}

    def peer(s):
        p = lax.rem(me + s, peers)
        return p, at(p)

    barrier = pltpu.get_barrier_semaphore()

    def greet(s):
        pl.semaphore_signal(barrier, inc=1, device_id=peer(s)[1], device_id_type=MESH)

    each(peers, greet)

    def by_expert(group, axis):
        to = lax.broadcasted_iota(jnp.int32, (group * ROWS, group * ROWS), axis)
        from_ = lax.broadcasted_iota(jnp.int32, (group * ROWS, group * ROWS), 1 - axis)
        slot = to % SLOTS
        image = (to // SLOTS) % group
        rest = to // (SLOTS * group)
        return one_hot(from_ == image * ROWS + rest * SLOTS + slot)

    group = max(g for g in range(1, 17) if peers % g == 0)
    sort = by_expert(group, 0)
    unsort = by_expert(group, 1)

    keys_copy.wait()
    keys = keys_v[...].astype(jnp.float32)
    unit = (keys * lax.rsqrt(jnp.sum(keys * keys, axis=1, keepdims=True) + 1e-06)).astype(
        jnp.bfloat16
    )
    x_copy.wait()
    weights = []
    for e in range(experts):
        for k, (hbm, vmem) in enumerate(((w_in_hbm, w_in_v), (w_out_hbm, w_out_v))):
            weights.append(
                pltpu.make_async_copy(hbm.at[e], vmem.at[e], local_sem.at[2 + 2 * e + k])
            )
    for copy in weights[0::2] + weights[1::2]:
        copy.start()

    x = x_v[...]
    logits = dot(unit, x, ((1,), (1,)))
    squares = None
    for start in range(0, width, LANES):
        floats = x[:, start : start + LANES].astype(jnp.float32)
        squares = floats * floats if squares is None else squares + floats * floats
    high = squares.astype(jnp.bfloat16)
    low = (squares - high.astype(jnp.float32)).astype(jnp.bfloat16)
    ones = jnp.ones((ROWS, LANES), jnp.bfloat16)
    total = dot(ones, high, ((1,), (1,))) + dot(ones, low, ((1,), (1,)))
    scale = 2.0 * lax.rsqrt(total[0:1] * (1.0 / width) + 1e-06)
    powers = jnp.exp(logits * scale)
    dispatch = (powers / jnp.sum(powers, axis=1, keepdims=True)).astype(jnp.bfloat16)
    slot_in = dot(dispatch, x)

    def message(values, first):
        return jnp.concatenate(
            [
                values[first : first + own, k * part : (k + 1) * part]
                for k in range(fold)
            ],
            axis=0,
        ).astype(jnp.bfloat16)

    for e in range(owners):
        send_in[e] = message(slot_in, e * own)
    pl.semaphore_wait(barrier, peers - 1)

    def far_first(j):
        h = lax.div(j, owners)
        h = jnp.where(2 * me_h < shares, shares - 1 - h, h)
        return h * owners + lax.rem(me_e + 1 + j, owners)

    def send_slots(j):
        p = far_first(j)

        @pl.when(p != me)
        def _():
            pltpu.make_async_remote_copy(
                src_ref=send_in.at[lax.rem(p, owners)],
                dst_ref=recv_in.at[me],
                send_sem=send_sem.at[0],
                recv_sem=recv_sem.at[0],
                device_id=at(p),
                device_id_type=MESH,
            ).start()

    send_slots(0)
    each(peers, send_slots)
    pltpu.make_async_copy(send_in.at[me_e], recv_in.at[me], recv_sem.at[0]).start()

    def arrival(buffer, sem, count):
        view = buffer.at[pl.ds(0, count)]
        return pltpu.make_async_copy(view, view, sem)

    block = group * ROWS
    span = group * SLOTS
    arrival(recv_in, recv_sem.at[0], peers).wait()
    starts = range(0, peers, group)
    sorted_rows = [
        dot(sort, recv_in[g : g + group].reshape(block, part)).astype(jnp.bfloat16)
        for g in starts
    ]
    partial = []
    for e in range(experts):
        weights[2 * e].wait()
        hidden = None
        for k in range(fold):
            at_row = (k * experts + e) * span
            rows = jnp.concatenate([r[at_row : at_row + span] for r in sorted_rows], axis=0)
            term = dot(rows, w_in_v[e, k * part : (k + 1) * part, :])
            hidden = term if hidden is None else hidden + term
        hidden = jax.nn.gelu(hidden, approximate=True).astype(jnp.bfloat16)
        weights[2 * e + 1].wait()
        partial.append(dot(hidden, w_out_v[e]).astype(jnp.bfloat16))
    for i, g in enumerate(starts):
        rows = jnp.concatenate(
            [
                partial[e][i * span : (i + 1) * span, k * part : (k + 1) * part]
                for k in range(fold)
                for e in range(experts)
            ],
            axis=0,
        )
        send_out[g : g + group] = (
            dot(unsort, rows).astype(jnp.bfloat16).reshape(group, ROWS, part)
        )

    def send_result(j):
        p = far_first(j)

        @pl.when(p != me)
        def _():
            pltpu.make_async_remote_copy(
                src_ref=send_out.at[p],
                dst_ref=recv_out.at[me],
                send_sem=send_sem.at[1],
                recv_sem=recv_sem.at[1],
                device_id=at(p),
                device_id_type=MESH,
            ).start()

    send_result(0)
    each(peers, send_result)

    combine = (powers / jnp.sum(powers, axis=0, keepdims=True)).astype(jnp.bfloat16)
    col = lax.broadcasted_iota(jnp.int32, (columns, peers * ROWS), 0)
    row = lax.broadcasted_iota(jnp.int32, (columns, peers * ROWS), 1)
    col_hit = col == ((row // ROWS) % owners) * own + row % own
    for k in range(fold):
        hit = jnp.logical_and(col_hit, (row // own) % fold == k)
        spread_v[k] = dot(combine, one_hot(hit), ((0,), (0,))).astype(jnp.bfloat16)

    pltpu.make_async_copy(send_out.at[me], recv_out.at[me], recv_sem.at[1]).start()
    arrival(recv_out, recv_sem.at[1], peers).wait()
    arrived = recv_out[...].reshape(peers * ROWS, part)
    for k in range(fold):
        out[0, :, k * part : (k + 1) * part] = dot(spread_v[k], arrived).astype(out.dtype)
    arrival(recv_in, send_sem.at[0], peers - 1).wait()
    arrival(send_out, send_sem.at[1], peers - 1).wait()


def body(images_in, slot_keys, w_in, w_out):
    owners = lax.axis_size("expert")
    shares = lax.axis_size("hid")
    peers = owners * shares
    _, tokens, width = images_in.shape
    own = w_in.shape[0] * SLOTS
    fold = ROWS // own
    part = width // fold
    hbm = pl.BlockSpec(memory_space=pltpu.HBM)
    bf16 = jnp.bfloat16
    return pl.pallas_call(
        functools.partial(kernel, owners, shares),
        out_shape=pltpu.VMEM(images_in.shape, bf16),
        in_specs=[hbm] * 4,
        out_specs=pl.BlockSpec(memory_space=pltpu.VMEM),
        scratch_shapes=[
            pltpu.VMEM((tokens, width), bf16),
            pltpu.VMEM(slot_keys.shape[::-1], bf16),
            pltpu.VMEM(w_in.shape, bf16),
            pltpu.VMEM(w_out.shape, bf16),
            pltpu.VMEM((owners, ROWS, part), bf16),
            pltpu.VMEM((peers, ROWS, part), bf16),
            pltpu.VMEM((peers, ROWS, part), bf16),
            pltpu.VMEM((peers, ROWS, part), bf16),
            pltpu.VMEM((fold, tokens, peers * ROWS), bf16),
            pltpu.SemaphoreType.DMA((2 + 2 * w_in.shape[0],)),
            pltpu.SemaphoreType.DMA((2,)),
            pltpu.SemaphoreType.DMA((2,)),
        ],
        compiler_params=pltpu.CompilerParams(
            collective_id=0, has_side_effects=True, vmem_limit_bytes=60 * 1024 * 1024
        ),
    )(images_in, slot_keys.T, w_in, w_out)


def solution(mesh):
    return jax.shard_map(
        body,
        mesh=mesh,
        in_specs=(
            P(("dp", "expert", "hid"), None, None),
            P(),
            P("expert", None, "hid"),
            P("expert", "hid", None),
        ),
        out_specs=P(("dp", "expert", "hid"), None, None),
        check_vma=False,
    )
```

```python
import functools

import jax
import jax.numpy as jnp
from jax import lax
from jax.experimental import pallas as pl
from jax.experimental.pallas import tpu as pltpu
from jax.sharding import PartitionSpec as P

SLOTS = 2
LANES = 128
ROWS = 16
MESH = pl.DeviceIdType.MESH


def each(count, step):
    if count <= 16:
        for s in range(1, count):
            step(s)
    else:

        def one(s, carry):
            step(s)
            return carry

        lax.fori_loop(1, count, one, 0)


def one_hot(hit):
    return jnp.where(hit, 1.0, 0.0).astype(jnp.bfloat16)


def dot(a, b, dims=((1,), (0,))):
    return lax.dot_general(a, b, (dims, ((), ())), preferred_element_type=jnp.float32)


def kernel(
    owners,
    shares,
    x_hbm,
    keys_hbm,
    w_in_hbm,
    w_out_hbm,
    out,
    x_v,
    keys_v,
    w_in_v,
    w_out_v,
    send_in,
    recv_in,
    send_out,
    recv_out,
    spread_v,
    local_sem,
    send_sem,
    recv_sem,
):
    peers = owners * shares
    tokens, width = x_v.shape
    experts, _, units = w_in_v.shape
    own = experts * SLOTS
    columns = keys_v.shape[0]
    fold = ROWS // own
    part = width // fold
    me_e = lax.axis_index("expert")
    me_h = lax.axis_index("hid")
    me = me_h * owners + me_e

    x_copy = pltpu.make_async_copy(x_hbm.at[0], x_v, local_sem.at[0])
    keys_copy = pltpu.make_async_copy(keys_hbm, keys_v, local_sem.at[1])
    x_copy.start()
    keys_copy.start()

    def at(p):
        return {"expert": lax.rem(p, owners), "hid": lax.div(p, owners)}

    def peer(s):
        p = lax.rem(me + s, peers)
        return p, at(p)

    barrier = pltpu.get_barrier_semaphore()

    def greet(s):
        pl.semaphore_signal(barrier, inc=1, device_id=peer(s)[1], device_id_type=MESH)

    each(peers, greet)

    weights = []
    for e in range(experts):
        for k, (hbm, vmem) in enumerate(((w_in_hbm, w_in_v), (w_out_hbm, w_out_v))):
            weights.append(
                pltpu.make_async_copy(hbm.at[e], vmem.at[e], local_sem.at[2 + 2 * e + k])
            )
    for copy in weights[0::2] + weights[1::2]:
        copy.start()

    def by_expert(group, axis):
        to = lax.broadcasted_iota(jnp.int32, (group * ROWS, group * ROWS), axis)
        from_ = lax.broadcasted_iota(jnp.int32, (group * ROWS, group * ROWS), 1 - axis)
        slot = to % SLOTS
        image = (to // SLOTS) % group
        rest = to // (SLOTS * group)
        return one_hot(from_ == image * ROWS + rest * SLOTS + slot)

    group = max(g for g in range(1, 17) if peers % g == 0)
    sort = by_expert(group, 0)
    unsort = by_expert(group, 1)

    keys_copy.wait()
    keys = keys_v[...].astype(jnp.float32)
    unit = (keys * lax.rsqrt(jnp.sum(keys * keys, axis=1, keepdims=True) + 1e-06)).astype(
        jnp.bfloat16
    )
    x_copy.wait()
    x = x_v[...]
    logits = dot(unit, x, ((1,), (1,)))
    squares = None
    for start in range(0, width, LANES):
        floats = x[:, start : start + LANES].astype(jnp.float32)
        squares = floats * floats if squares is None else squares + floats * floats
    high = squares.astype(jnp.bfloat16)
    low = (squares - high.astype(jnp.float32)).astype(jnp.bfloat16)
    ones = jnp.ones((ROWS, LANES), jnp.bfloat16)
    total = dot(ones, high, ((1,), (1,))) + dot(ones, low, ((1,), (1,)))
    scale = 2.0 * lax.rsqrt(total[0:1] * (1.0 / width) + 1e-06)
    powers = jnp.exp(logits * scale)
    dispatch = (powers / jnp.sum(powers, axis=1, keepdims=True)).astype(jnp.bfloat16)
    slot_in = dot(dispatch, x)

    def message(values, first):
        return jnp.concatenate(
            [
                values[first : first + own, k * part : (k + 1) * part]
                for k in range(fold)
            ],
            axis=0,
        ).astype(jnp.bfloat16)

    for e in range(owners):
        send_in[e] = message(slot_in, e * own)
    pl.semaphore_wait(barrier, peers - 1)

    def far_first(j):
        h = lax.div(j, owners)
        h = jnp.where(2 * me_h < shares, shares - 1 - h, h)
        return h * owners + lax.rem(me_e + 1 + j, owners)

    def send_slots(j):
        p = far_first(j)

        @pl.when(p != me)
        def _():
            pltpu.make_async_remote_copy(
                src_ref=send_in.at[lax.rem(p, owners)],
                dst_ref=recv_in.at[me],
                send_sem=send_sem.at[0],
                recv_sem=recv_sem.at[0],
                device_id=at(p),
                device_id_type=MESH,
            ).start()

    send_slots(0)
    each(peers, send_slots)
    pltpu.make_async_copy(send_in.at[me_e], recv_in.at[me], recv_sem.at[0]).start()

    def arrival(buffer, sem, count):
        view = buffer.at[pl.ds(0, count)]
        return pltpu.make_async_copy(view, view, sem)

    block = group * ROWS
    span = group * SLOTS
    for copy in weights:
        copy.wait()
    arrival(recv_in, recv_sem.at[0], peers).wait()
    starts = range(0, peers, group)
    sorted_rows = [
        dot(sort, recv_in[g : g + group].reshape(block, part)).astype(jnp.bfloat16)
        for g in starts
    ]
    partial = []
    hiddens = []
    for e in range(experts):
        hidden = None
        for k in range(fold):
            at_row = (k * experts + e) * span
            rows = jnp.concatenate([r[at_row : at_row + span] for r in sorted_rows], axis=0)
            term = dot(rows, w_in_v[e, k * part : (k + 1) * part, :])
            hidden = term if hidden is None else hidden + term
        hidden = jax.nn.gelu(hidden, approximate=True).astype(jnp.bfloat16)
        hiddens.append(hidden)
    for e in range(experts):
        partial.append(dot(hiddens[e], w_out_v[e]).astype(jnp.bfloat16))
    for i, g in enumerate(starts):
        rows = jnp.concatenate(
            [
                partial[e][i * span : (i + 1) * span, k * part : (k + 1) * part]
                for k in range(fold)
                for e in range(experts)
            ],
            axis=0,
        )
        send_out[g : g + group] = (
            dot(unsort, rows).astype(jnp.bfloat16).reshape(group, ROWS, part)
        )

    def send_result(s):
        p = lax.rem(me + s, peers)
        pltpu.make_async_remote_copy(
            src_ref=send_out.at[p],
            dst_ref=recv_out.at[me],
            send_sem=send_sem.at[1],
            recv_sem=recv_sem.at[1],
            device_id=at(p),
            device_id_type=MESH,
        ).start()

    each(peers, send_result)

    combine = (powers / jnp.sum(powers, axis=0, keepdims=True)).astype(jnp.bfloat16)
    col = lax.broadcasted_iota(jnp.int32, (columns, peers * ROWS), 0)
    row = lax.broadcasted_iota(jnp.int32, (columns, peers * ROWS), 1)
    col_hit = col == ((row // ROWS) % owners) * own + row % own
    for k in range(fold):
        hit = jnp.logical_and(col_hit, (row // own) % fold == k)
        spread_v[k] = dot(combine, one_hot(hit), ((0,), (0,))).astype(jnp.bfloat16)

    pltpu.make_async_copy(send_out.at[me], recv_out.at[me], recv_sem.at[1]).start()
    arrival(recv_out, recv_sem.at[1], peers).wait()
    arrived = recv_out[...].reshape(peers * ROWS, part)
    for k in range(fold):
        out[0, :, k * part : (k + 1) * part] = dot(spread_v[k], arrived).astype(out.dtype)
    arrival(recv_in, send_sem.at[0], peers - 1).wait()
    arrival(send_out, send_sem.at[1], peers - 1).wait()


def body(images_in, slot_keys, w_in, w_out):
    owners = lax.axis_size("expert")
    shares = lax.axis_size("hid")
    peers = owners * shares
    _, tokens, width = images_in.shape
    own = w_in.shape[0] * SLOTS
    fold = ROWS // own
    part = width // fold
    hbm = pl.BlockSpec(memory_space=pltpu.HBM)
    bf16 = jnp.bfloat16
    return pl.pallas_call(
        functools.partial(kernel, owners, shares),
        out_shape=pltpu.VMEM(images_in.shape, bf16),
        in_specs=[hbm] * 4,
        out_specs=pl.BlockSpec(memory_space=pltpu.VMEM),
        scratch_shapes=[
            pltpu.VMEM((tokens, width), bf16),
            pltpu.VMEM(slot_keys.shape[::-1], bf16),
            pltpu.VMEM(w_in.shape, bf16),
            pltpu.VMEM(w_out.shape, bf16),
            pltpu.VMEM((owners, ROWS, part), bf16),
            pltpu.VMEM((peers, ROWS, part), bf16),
            pltpu.VMEM((peers, ROWS, part), bf16),
            pltpu.VMEM((peers, ROWS, part), bf16),
            pltpu.VMEM((fold, tokens, peers * ROWS), bf16),
            pltpu.SemaphoreType.DMA((2 + 2 * w_in.shape[0],)),
            pltpu.SemaphoreType.DMA((2,)),
            pltpu.SemaphoreType.DMA((2,)),
        ],
        compiler_params=pltpu.CompilerParams(
            collective_id=0, has_side_effects=True, vmem_limit_bytes=60 * 1024 * 1024
        ),
    )(images_in, slot_keys.T, w_in, w_out)


def solution(mesh):
    return jax.shard_map(
        body,
        mesh=mesh,
        in_specs=(
            P(("dp", "expert", "hid"), None, None),
            P(),
            P("expert", None, "hid"),
            P("expert", "hid", None),
        ),
        out_specs=P(("dp", "expert", "hid"), None, None),
        check_vma=False,
    )
```
